256 devices in a mesh: dp: 32 (over z, y), tensor: 8 (over x, core).
Axes of the slice: x: 4, y: 4, z: 8, core: 2. Of those that a mesh axis runs over, the one named last changes fastest.
Arguments:
- hidden: bfloat16 [128, 256, 4096], P('dp'), may hold values from -6 to 6
- lengths: int32 [128], P('dp'), may hold values from 1 to 256, 19660 in all
- judge: bfloat16 [512, 16, 4096], P('dp', None, 'tensor'), may hold values from -6 to 6
- w_query: bfloat16 [4096, 4096], P(None, 'tensor'), may hold values from -0.09375 to 0.09375
- w_keyval: bfloat16 [4096, 2048], P(None, 'tensor'), may hold values from -0.09375 to 0.09375
- pair_devices: int32 [512, 2], P('dp'), may hold values from 0 to 31, as said below
- pair_items: int32 [512, 2], P('dp'), may hold values from 0 to 3, as said below
Outputs:
- encoded: bfloat16 [128, 256, 4096], P('dp', None, 'tensor')
- pair_attended: bfloat16 [512, 16, 4096], P('dp', None, 'tensor')
The draws below stay inside these ranges and needn't reach their ends.
Inputs may be any that keep to these rules, and one draw needn't show every extreme that they name: `pair_devices`: each prompt's responses are spread over a band of 8 consecutive dp indices, so that their ragged lengths share the load: index 8 b + k holds at place i the k-th response of band b's prompt i. The two sides of a pair are two responses of one prompt (same band, same place, different indices). In each aligned block of 16 rows (the pairs of one dp index) no index is named more than 2 times, and some index exactly 2 times. `pair_items`: both sides of a pair have the same place.
All inputs are finite; a program needn't handle non-finite values. No bound on the sum of `lengths` on one device may be relied on, other than what follows from the above.
Results may differ from the reference program's by a relative error of at most 0.0069.
Values may be sent and summed in bfloat16 or wider, within the bound.
A program may use at most 128 MiB of HBM per device.

```python
import math
import jax
import jax.numpy as jnp
import numpy as np
from jax import lax

D = 4096
H = 32
KVH = 8
HD = 128
L = 256
M = 16
RESP_DEV = 4
PAIR_DEV = 16
CAP = 2
R = 128
PAIRS = 512
N_DP = 32


def pair_layout(key):
    blocks = PAIRS // PAIR_DEV
    matches = PAIR_DEV // 4
    band_count = N_DP // 8
    key_band, key_prompt, key_order = jax.random.split(key, 3)
    offsets = jax.random.permutation(key_band, jnp.arange(blocks, dtype=jnp.int32) % band_count)
    group_of = jnp.arange(matches, dtype=jnp.int32) // CAP
    band_of = (offsets[:, None] + group_of[None, :]) % band_count
    prompts = jax.random.permutation(key_prompt, jnp.arange(blocks * matches, dtype=jnp.int32) % RESP_DEV)
    prompts = prompts.reshape(blocks, matches)
    order_keys = jax.random.split(key_order, blocks * matches)
    orders = jax.vmap(lambda single: jax.random.permutation(single, 8))(order_keys).astype(jnp.int32)
    orders = orders.reshape(blocks, matches, 4, 2)
    devices = band_of[:, :, None, None] * 8 + orders
    places = jnp.broadcast_to(prompts[:, :, None, None], orders.shape)
    return (devices.reshape(PAIRS, 2).astype(jnp.int32), places.reshape(PAIRS, 2).astype(jnp.int32))


def draw_pair_devices(key, part):
    devices, places = pair_layout(key)
    return devices


def draw_pair_items(key, part):
    devices, places = pair_layout(key)
    return places


def block_scale(own_key, shape, cuts, least, largest):
    def one(position, shards_of):
        steps = jax.random.uniform(jax.random.fold_in(jax.random.fold_in(own_key, 6), position), (shards_of,), jnp.float32, least / len(cuts), largest / len(cuts))
        return jnp.repeat(jnp.exp(steps), shape[position] // shards_of).reshape((-1,) + (1,) * (len(shape) - position - 1))

    loudness = one(*cuts[0])
    for cut in cuts[1:]:
        loudness = loudness * one(*cut)
    return loudness


def length_profile(count, total, bound, slope):
    portions = [(1 << 20) // math.isqrt(grade ** slope) + 1 for grade in range(2, count + 1)]
    surplus, counts = total - bound - (count - 1), [1] * (count - 1)
    while surplus > 0:
        movable = [i for i in range(count - 1) if counts[i] < bound]
        mass, left = sum([portions[i] for i in movable]), surplus
        for i in movable:
            addition = min(bound - counts[i], max(1, left * portions[i] // mass), surplus)
            counts[i] = counts[i] + addition
            surplus = surplus - addition
    return np.array([bound] + counts)


def ragged_sizes(own_key, count, total, most, lean):
    if count == 2:
        one = jax.random.randint(own_key, (), max(1, total - most), min(most, total - 1) + 1)
        return jnp.stack([one, total - one])
    tallies = jnp.asarray(length_profile(count, total, most, lean), jnp.int32)
    twos = (count - 1) // 2
    donor, taker = tallies[1:1 + 2 * twos:2], tallies[2:2 + 2 * twos:2]
    slack = jnp.minimum(donor - 1, most - taker)
    passed = jax.random.randint(jax.random.fold_in(own_key, 1), (twos,), 0, 1 << 20) % (slack + 1)
    tallies = tallies.at[1:1 + 2 * twos:2].set(donor - passed).at[2:2 + 2 * twos:2].set(taker + passed)
    return tallies[jax.random.permutation(jax.random.fold_in(own_key, 2), count)]


def centred(stream_key, extent, deviation, limit, shards=(), held_as=jnp.bfloat16):
    drawn = jax.random.normal(stream_key, extent, jnp.float32) * deviation
    if len(shards) > 0:
        drawn = block_scale(stream_key, extent, shards, -0.22, 0.18) * drawn
    return jnp.clip(drawn, min=-limit, max=limit).astype(held_as)


def setup_inputs(seed: int = 0) -> dict:
    key_of = jax.random.split(jax.random.key(seed), 8)
    return {
        "hidden": centred(key_of[0], (R, L, D), 1.0, 6.0, ((0, 32),)),
        "lengths": ragged_sizes(key_of[1], R, R * L * 3 // 5, L, 2).astype(jnp.int32),
        "judge": centred(key_of[2], (PAIRS, M, D), 1.0, 6.0, ((0, 32), (2, 8))),
        "w_query": centred(key_of[3], (D, H * HD), D ** -0.5, 0.09375, ((1, 8),)),
        "w_keyval": centred(key_of[4], (D, 2 * KVH * HD), D ** -0.5, 0.09375, ((1, 8),)),
        "pair_devices": draw_pair_devices(jax.random.fold_in(key_of[7], 71), 0),
        "pair_items": draw_pair_items(jax.random.fold_in(key_of[7], 71), 0),
    }


softcap_limit = 5.0


def capped(scores):
    return softcap_limit * jnp.tanh(scores / softcap_limit)


def widened(values):
    return lax.optimization_barrier(values.astype(jnp.bfloat16)).astype(jnp.float32)


def reference(hidden, lengths, judge, w_query, w_keyval, pair_devices, pair_items):
    group = H // KVH
    scale = HD ** -0.5
    positions = jnp.arange(L, dtype=jnp.int32)

    def encode(packed):
        tokens, length = packed
        queries = jnp.dot(tokens, w_query, preferred_element_type=jnp.float32)
        keyval = jnp.dot(tokens, w_keyval, preferred_element_type=jnp.float32).astype(jnp.bfloat16)
        split = lax.optimization_barrier(keyval).astype(jnp.float32).reshape(L, KVH, 2, HD)
        q_heads = widened(queries).reshape(L, KVH, group, HD)
        scores = capped(jnp.einsum('qkgd,tkd->kgqt', q_heads, split[:, :, 0]) * scale)
        allowed = (positions[None, :] <= positions[:, None]) & (positions[None, :] < length)
        weights = jnp.where(allowed, jnp.exp(scores), 0.0)
        probs = widened(weights / jnp.sum(weights, -1, keepdims=True))
        attended = jnp.einsum('kgqt,tkd->qkgd', probs, split[:, :, 1])
        return attended.reshape(L, H * HD).astype(jnp.bfloat16), keyval

    encoded, keyvals = lax.map(encode, (hidden, lengths))
    judge_q = widened(jnp.dot(judge.reshape(PAIRS * M, D), w_query, preferred_element_type=jnp.float32))
    judge_q = judge_q.reshape(PAIRS, M, KVH, group, HD)
    resp_ids = (pair_devices * RESP_DEV + pair_items).astype(jnp.int32)

    def score(packed):
        queries, ids = packed
        total_out = jnp.zeros((M, KVH, group, HD), jnp.float32)
        total_sum = jnp.zeros((KVH, group, M), jnp.float32)
        for side in range(2):
            keyval = keyvals[ids[side]].astype(jnp.float32).reshape(L, KVH, 2, HD)
            scores = capped(jnp.einsum('mkgd,tkd->kgmt', queries, keyval[:, :, 0]) * scale)
            weights = jnp.where(positions < lengths[ids[side]], jnp.exp(scores), 0.0)
            total_sum = total_sum + jnp.sum(weights, -1)
            total_out = total_out + jnp.einsum('kgmt,tkd->mkgd', widened(weights), keyval[:, :, 1])
        normal = total_out / jnp.transpose(total_sum, (2, 0, 1))[..., None]
        return normal.reshape(M, H * HD).astype(jnp.bfloat16)

    pair_attended = lax.map(score, (judge_q, resp_ids))
    return encoded, pair_attended
```

```python
import functools
import math
import jax
import jax.numpy as jnp
from jax import lax
from jax.experimental import pallas as pl
from jax.experimental.pallas import tpu as pltpu
from jax.sharding import PartitionSpec as P

HD = 128
C = 4
BF = jnp.bfloat16
F32 = jnp.float32
I32 = jnp.int32
MESH = pl.DeviceIdType.MESH
CAP_IN = HD ** -0.5 / 5.0
CAP_OUT = 5.0 * math.log2(math.e)

SCHED = (
    "KV0", "KV1", "KV2", "KV3", "XF0", "MY", "Q0", "MR", "Z0", "QP0",
    "XF1", "Y00", "Q1", "Z1", "QP1", "ML", "Y10", "XF2", "Q2", "MW",
    "Z2", "QP2", "Y20", "XF3", "Q3", "Z3", "QP3", "Y30", "VP", "A00",
    "Y03", "Y02", "Y01", "A10", "R00", "A20", "Y13", "Y12", "Y11", "A30",
    "A03", "Y23", "Y22", "Y21", "A02", "R10", "R20", "Y33", "A01", "Y32",
    "Y31", "A13", "R30", "A12", "R03", "A11", "SA0", "A23", "A22", "R02",
    "A21", "R01", "A33", "A32", "R13", "R12", "A31", "SA1", "R11", "R23",
    "R22", "SA2", "R21", "R33", "R32", "SA3", "R31", "H",
)


def weights_of(scores):
    return jnp.exp2(jnp.tanh(scores * CAP_IN) * CAP_OUT)


def kernel(judge, hidden, wq, wkv, lens, pdev, pitem, enc, pair, *scratch):
    (hid_v, wq_v, wkv_v, jin, jb, qself, kvx, vext, zs, ys, yq, rs, zr, mt, sm, smr, sm0, lt, ls,
     oenc, opair, lsem, ssem, rsem, qb, zq, yr, hret) = scratch
    npair, ntok, kslice = judge.shape
    tc = ntok // C
    rows = tc * 4
    per = rows // 16
    dp = lax.axis_index("dp")
    t = lax.axis_index("tensor")
    z, y = dp // 4, lax.rem(dp, 4)
    x, core = t // 2, lax.rem(t, 2)
    odd = lax.rem(z, 2)
    sg = 2 * odd - 1
    band = z // 2

    def mod(a, n):
        return lax.rem(a + 4 * n, n)

    zt = [z, mod(z + sg, 8), mod(z - 2 * sg, 8), mod(z + 3 * sg, 8)]
    zh = [z] + [mod(z + n * sg, 8) for n in (1, 2, 3)]

    def at(zz=None, yy=None, xx=None, cc=None):
        zz, yy = (z if zz is None else zz), (y if yy is None else yy)
        xx, cc = (x if xx is None else xx), (core if cc is None else cc)
        return (zz * 4 + yy, xx * 2 + cc)

    local_count = [0]
    recv_of, send_of, finals = {}, {}, []

    def remote(name, src, dst, dev, group, total):
        if group not in send_of:
            send_of[group] = len(send_of)
            finals.append((send_of[group], total))
        if name not in recv_of:
            recv_of[name] = len(recv_of)
        pltpu.make_async_remote_copy(
            src_ref=src, dst_ref=dst, send_sem=ssem.at[send_of[group]], recv_sem=rsem.at[recv_of[name]],
            device_id=dev, device_id_type=MESH).start()

    def arrived(name, dst):
        if name not in recv_of:
            recv_of[name] = len(recv_of)
        pltpu.make_async_remote_copy(
            src_ref=dst, dst_ref=dst, send_sem=ssem.at[0], recv_sem=rsem.at[recv_of[name]],
            device_id=(dp, t), device_id_type=MESH).wait_recv()

    def local(src, dst):
        copy = pltpu.make_async_copy(src, dst, lsem.at[local_count[0]])
        local_count[0] += 1
        copy.start()
        return copy

    l_j = local(judge, jin)
    l_kv = local(wkv, wkv_v)
    l_h = [local(hidden.at[0], hid_v.at[0]), local(hidden.at[1], hid_v.at[1])]
    l_q = local(wq, wq_v)
    l_h += [local(hidden.at[2], hid_v.at[2]), local(hidden.at[3], hid_v.at[3])]

    barrier = pltpu.get_barrier_semaphore()
    peers = [at(xx=mod(x + d, 4)) for d in (1, 2, 3)] + [at(cc=1 - core)]
    peers += [at(yy=mod(y + d, 4)) for d in (1, 2, 3)]
    peers += [at(zz=mod(z + d, 8)) for d in (1, -1, 2, -2, 3, -3)]
    for dev in peers:
        pl.semaphore_signal(barrier, inc=1, device_id=dev, device_id_type=MESH)

    l_j.wait()
    for c in range(C):
        part = jin[...].astype(F32)[:, c * tc:(c + 1) * tc, :]
        jb[c, t] = part.reshape(npair * tc, kslice).astype(BF)

    pl.semaphore_wait(barrier, len(peers))

    xl, xr, x2 = mod(x - 1, 4), mod(x + 1, 4), mod(x + 2, 4)
    sl, sr, s2 = xl * 2 + core, xr * 2 + core, x2 * 2 + core
    sib = at(cc=1 - core)

    def xsend(name, c, slot, dev):
        remote(f"{name}{c}", jb.at[c, slot], jb.at[c, slot], dev, f"x{c}", jb.at[c, pl.ds(0, 7)])

    def X0(c):
        xsend("x2", c, t, at(xx=x2))
        xsend("xl", c, t, at(xx=xr))
        xsend("xr", c, t, at(xx=xl))
        xsend("sb", c, t, sib)

    def XF(c):
        for name, slot in (("xl", sl), ("xr", sr), ("x2", s2)):
            arrived(f"{name}{c}", jb.at[c, slot])
            xsend("sb", c, slot, sib)

    def piece(c, i):
        return jnp.dot(jb[c, i], wq_v[pl.ds(pl.multiple_of(i * kslice, kslice), kslice), :],
                       preferred_element_type=F32)

    def Q(c):
        q = piece(c, t) + piece(c, sl) + piece(c, sr) + piece(c, s2)
        arrived(f"sb{c}", jb.at[c, pl.ds(0, 4)])
        for slot in (t, sl, sr, s2):
            q = q + piece(c, slot + 1 - 2 * core)
        heads = [q[:, h * HD:(h + 1) * HD].reshape(npair, tc, HD) for h in range(4)]
        qb[c][...] = jnp.concatenate(heads, 1).astype(BF)

    def MZ():
        for n in (1, 2, 3):
            remote("mz", mt.at[y, 0], mt.at[y, n], at(zz=zt[n]), "mz", mt.at[y, pl.ds(0, 3)])
        remote("len", lt.at[odd], lt.at[odd], at(zz=z + 1 - 2 * odd), "len", lt.at[odd])

    late = []

    def MY():
        arrived("mz", mt.at[y, pl.ds(1, 3)])
        for d in (1, 2, 3):
            remote("my", mt.at[y], mt.at[y], at(yy=mod(y + d, 4)), "my", mt.at[pl.ds(0, 3)])
        late.append(local(mt.at[y], smr))

    def ML():
        arrived("my", mt.at[pl.ds(0, 3)])
        arrived("len", lt.at[1 - odd])
        late.append(local(mt, sm))
        late.append(local(lt, ls))

    def MR():
        late[0].wait()

    def MW():
        late[1].wait()
        late[2].wait()

    def masked(v, length):
        keys = lax.broadcasted_iota(I32, (v.shape[0], 2 * HD), 0)
        both = jnp.concatenate([v.astype(F32), jnp.ones(v.shape, F32)], 1)
        return jnp.where(keys < length, both, 0.0).astype(BF)

    def KV(r):
        if r == 0:
            l_kv.wait()
        l_h[r].wait()
        kv = jnp.dot(hid_v[r], wkv_v[...], preferred_element_type=F32).astype(BF)
        kvx[odd, r, 0] = kv[:, :HD]
        kvx[odd, r, 1] = kv[:, HD:]
        vext[odd, r] = masked(kv[:, HD:], lens[r])
        remote("kv", kvx.at[odd, r], kvx.at[odd, r], at(zz=z + 1 - 2 * odd),
               "kv", kvx.at[odd])

    def VP():
        other = 1 - odd
        arrived("kv", kvx.at[other])

        def one(r, carry):
            vext[other, r] = masked(kvx[other, r, 1], ls[other, 0, r])
            return carry

        lax.fori_loop(0, 4, one, 0)

    def QP(r):
        q = jnp.dot(hid_v[r], wq_v[...], preferred_element_type=F32).astype(BF)
        for h in range(4):
            qself[r, h] = q[:, h * HD:(h + 1) * HD]

    enc_out = []

    def SA(r):
        k_r = kvx[odd, r, 0]
        v_r = vext[odd, r]
        for h in range(4):
            for b in range(2):
                n = (b + 1) * 128
                s = lax.dot_general(qself[r, h, b * 128:(b + 1) * 128, :], k_r[:n],
                                    (((1,), (1,)), ((), ())), preferred_element_type=F32)
                qi = lax.broadcasted_iota(I32, (128, n), 0) + b * 128
                ti = lax.broadcasted_iota(I32, (128, n), 1)
                w = jnp.where(ti <= qi, weights_of(s), 0.0).astype(BF)
                ne = jnp.dot(w, v_r[:n], preferred_element_type=F32)
                oenc[r, b * 128:(b + 1) * 128, h * HD:(h + 1) * HD] = (
                    ne[:, :HD] / ne[:, HD:]).astype(BF)
        enc_out.append(local(oenc.at[r], enc.at[r]))

    def Z(c):
        for n in (3, 2, 1, 0):
            for k in range(8):
                block = qb[c][jnp.bitwise_and(sm0[4, n * 8 + k], npair - 1)]
                if n:
                    zs[c, n - 1, k] = block
                else:
                    zq[c][0][k] = block
            if n:
                remote(f"z{c}{n}", zs.at[c, n - 1], zq[c][n], at(zz=zt[n]), f"z{c}", zs.at[c])

    def Y(c, n):
        if n:
            arrived(f"z{c}{n}", zq[c][n])
        tile = smr.at[n] if n else sm0
        for d in (2, 1, 3, 0):
            yy = mod(y + d, 4)
            for s in range(4):
                which = jnp.bitwise_and(tile[s % 2, (2 * band + s // 2) * 4 + yy], 7)
                block = zq[c][n][which]
                if d:
                    ys[c, n, d - 1, s] = block
                else:
                    yq[c, n, y, s] = block
            if d:
                remote(f"y{c}{n}", ys.at[c, n, d - 1], yq.at[c, n, y], at(yy=yy), f"y{c}", ys.at[c])

    diag = lax.broadcasted_iota(I32, (rows, 128), 0) == lax.broadcasted_iota(I32, (rows, 128), 1)
    sub16 = lax.broadcasted_iota(I32, (16, 128), 0)

    def A(c, n):
        arrived(f"y{c}{n}", yq.at[c, n, pl.ds(0, 3)])

        def one(src, carry):
            dens = []
            for s in range(4):
                zz, j = s // 2, s % 2
                it = jnp.bitwise_and(sm[src, n, 2 + j, (2 * band + zz) * 4 + y], 3)
                sc = lax.dot_general(yq[c, n, src, s], kvx[zz, it, 0],
                                     (((1,), (1,)), ((), ())), preferred_element_type=F32)
                ne = jnp.dot(weights_of(sc).astype(BF), vext[zz, it], preferred_element_type=F32)
                rs[c, n, src, s * per:(s + 1) * per] = ne[:, :HD].astype(BF).reshape(per, 16, HD)
                dens.append(jnp.sum(jnp.where(diag, ne[:, HD:], 0.0), 0, keepdims=True))
            den = jnp.concatenate(dens, 0)
            high = den.astype(BF).astype(F32)
            rs[c, n, src, 4 * per] = jnp.concatenate(
                [high, den - high, jnp.zeros((8, 128), F32)], 0).astype(BF)
            return carry

        lax.fori_loop(0, 4, one, 0, unroll=4)
        for d in (2, 1, 3):
            yy = mod(y + d, 4)
            remote(f"r{c}{n}", rs.at[c, n, yy], yr[c][n].at[y], at(yy=yy), f"r{c}", rs.at[c, pl.ds(0, 3)])
        yr[c][n][y] = rs[c, n, y]

    def R(c, n):
        arrived(f"r{c}{n}", yr[c][n].at[pl.ds(0, 3)])
        tile = smr.at[n] if n else sm0
        for k in range(8):
            num, den = [], []
            for side in (0, 1):
                p = jnp.bitwise_and(tile[5 + side, n * 8 + k], 15)
                src, s = p // 4, lax.rem(p, 4)
                num.append(yr[c][n][src, pl.ds(s * per, per)].reshape(rows, HD).astype(F32))
                dens = yr[c][n][src, 4 * per].astype(F32)
                den.append(jnp.where((sub16 == s) | (sub16 == s + 4), dens, 0.0))
            total = jnp.sum(den[0] + den[1], 0, keepdims=True)
            total = jnp.sum(jnp.where(diag, total, 0.0), 1, keepdims=True)
            block = ((num[0] + num[1]) / total).astype(BF)
            if n:
                zr[c, n - 1, k] = block
            else:
                hret[c][k] = block
        if n:
            remote(f"h{c}", zr.at[c, n - 1], hret[c].at[pl.ds(n * 8, 8)], at(zz=zh[n]), f"h{c}", zr.at[c])

    def H():
        for c in range(C):
            arrived(f"h{c}", hret[c].at[pl.ds(8, 24)])
        for p in range(npair):
            spot_p = jnp.bitwise_and(sm0[7, p], 31)
            got = [hret[c][spot_p].astype(F32) for c in range(C)]
            for h in range(4):
                opair[p, :, h * HD:(h + 1) * HD] = jnp.concatenate(
                    [g[h * tc:(h + 1) * tc] for g in got], 0).astype(BF)
        enc_out.append(local(opair, pair))

    for c in range(C):
        X0(c)

    lane = lax.broadcasted_iota(I32, (npair, 128), 1)
    sub = lax.broadcasted_iota(I32, (npair, 128), 0)
    eye = lax.broadcasted_iota(I32, (npair, npair), 0) == lax.broadcasted_iota(I32, (npair, npair), 1)

    def column(row):
        return jnp.sum(jnp.where(eye, row, 0), 1, keepdims=True)

    dev0, dev1, item = column(pdev[0:1, :]), column(pdev[1:2, :]), column(pitem[0:1, :])
    strict = jnp.where(
        lax.broadcasted_iota(I32, (npair, npair), 1) < lax.broadcasted_iota(I32, (npair, npair), 0),
        1.0, 0.0).astype(F32)
    m0 = jnp.where(dev0 == lane, 1.0, 0.0)
    m1 = jnp.where(dev1 == lane, 1.0, 0.0)
    m = m0 + m1
    rank = jnp.dot(strict, m, preferred_element_type=F32)
    rel = jnp.bitwise_and(lax.shift_right_logical(dev0, 3) - band + 4, 3)
    near = jnp.where(rel == 0, 0, jnp.where(rel == 2, 3, jnp.where((rel == 1) == (odd == 1), 1, 2)))
    mb = jnp.where(near == lane, 1.0, 0.0)
    place = jnp.sum(mb * jnp.dot(strict, mb, preferred_element_type=F32), 1, keepdims=True)
    home = near.astype(F32) * 8.0 + place
    at_home = jnp.where(home == lane.astype(F32), 1.0, 0.0)

    def down(v):
        return jnp.sum(v, 0, keepdims=True)

    first = jnp.where(rank == 0.0, m, 0.0)
    second = jnp.where(rank == 1.0, m, 0.0)
    spot = (jnp.bitwise_and(lane, 3) * 4
            + jnp.bitwise_and(lax.shift_right_logical(lane, 2), 1) * 2).astype(F32) + rank
    pos0 = jnp.sum(m0 * spot, 1, keepdims=True)
    pos1 = jnp.sum(m1 * spot, 1, keepdims=True)
    itemf = item.astype(F32)
    subf = sub.astype(F32)
    table = jnp.concatenate([
        down(first * place), down(second * place), down(first * itemf), down(second * itemf),
        down(at_home * subf), down(at_home * pos0), down(at_home * pos1),
        down(jnp.where(sub == lane, home, 0.0))], 0)
    mt[y, 0] = table.astype(I32)
    l_0 = local(mt.at[y, 0], sm0)
    lane8 = lax.broadcasted_iota(I32, (8, 128), 1)
    lt[odd] = jnp.where(lane8 == 0, lens[0], jnp.where(lane8 == 1, lens[1],
                        jnp.where(lane8 == 2, lens[2], lens[3])))

    MZ()
    stages = {"XF": XF, "MR": MR, "MW": MW, "Q": Q, "KV": KV, "QP": QP, "SA": SA, "Z": Z, "Y": Y, "A": A,
              "R": R, "MY": MY, "ML": ML, "VP": VP, "H": H}
    waited = []
    for word in SCHED:
        name = word.rstrip("0123456789")
        if name in ("Q", "QP") and not waited:
            l_q.wait()
            l_0.wait()
            waited.append(word)
        stages[name](*[int(d) for d in word[len(name):]])
    for copy in enc_out:
        copy.wait()
    for slot, total in finals:
        pltpu.make_async_remote_copy(
            src_ref=total, dst_ref=total, send_sem=ssem.at[slot], recv_sem=rsem.at[0],
            device_id=(dp, t), device_id_type=MESH).wait_send()


def copy_kernel(enc, pair, enc_out, pair_out, enc_v, pair_v, sem):
    steps = [(enc.at[r], enc_v.at[r], enc_out.at[r]) for r in range(4)] + [(pair, pair_v, pair_out)]
    inward = [pltpu.make_async_copy(src, mid, sem.at[k]) for k, (src, mid, _) in enumerate(steps)]
    outward = [pltpu.make_async_copy(mid, dst, sem.at[5 + k]) for k, (_, mid, dst) in enumerate(steps)]
    for copy in inward:
        copy.start()
    for first, second in zip(inward, outward):
        first.wait()
        second.start()
    for copy in outward:
        copy.wait()


def copied(encoded, attended):
    spec = pl.BlockSpec(memory_space=pl.ANY)
    return pl.pallas_call(
        copy_kernel,
        out_shape=[jax.ShapeDtypeStruct(a.shape, a.dtype) for a in (encoded, attended)],
        in_specs=[spec, spec], out_specs=[spec, spec],
        scratch_shapes=[pltpu.VMEM(encoded.shape, BF), pltpu.VMEM(attended.shape, BF),
                        pltpu.SemaphoreType.DMA((10,))],
        name="results",
    )(encoded, attended)


def on_device(hidden, lengths, judge, w_query, w_keyval, pair_devices, pair_items):
    npair, ntok, kslice = judge.shape
    nresp, seq, width = hidden.shape
    rows = ntok // C * 4
    V = pltpu.VMEM
    scratch = [
        V((nresp, seq, width), BF), V(w_query.shape, BF), V(w_keyval.shape, BF), V(judge.shape, BF),
        V((C, 8, npair * ntok // C, kslice), BF), V((nresp, 4, seq, HD), BF),
        V((2, 4, 2, seq, HD), BF), V((2, 4, seq, 2 * HD), BF),
        V((C, 3, 8, rows, HD), BF), V((C, 4, 3, 4, rows, HD), BF), V((C, 4, 4, 4, rows, HD), BF),
        V((C, 4, 4, rows // 4 + 1, 16, HD), BF), V((C, 3, 8, rows, HD), BF),
        V((4, 4, 8, 128), I32), pltpu.SMEM((4, 4, 8, 128), I32), pltpu.SMEM((4, 8, 128), I32), pltpu.SMEM((8, 128), I32),
        V((2, 8, 128), I32), pltpu.SMEM((2, 8, 128), I32),
        V((nresp, seq, 4 * HD), BF), V((npair, ntok, 4 * HD), BF),
        pltpu.SemaphoreType.DMA((16,)), pltpu.SemaphoreType.DMA((5 * C + 4,)), pltpu.SemaphoreType.DMA((16 * C + 4,)),
        [V((npair, rows, HD), BF) for _ in range(C)],
        [[V((8, rows, HD), BF) for _ in range(4)] for _ in range(C)],
        [[V((4, rows // 4 + 1, 16, HD), BF) for _ in range(4)] for _ in range(C)],
        [V((32, rows, HD), BF) for _ in range(C)],
    ]
    flat, tree = jax.tree.flatten(scratch, is_leaf=lambda s: not isinstance(s, list))

    def body(*refs):
        nested = jax.tree.unflatten(tree, refs[9:])
        kernel(*refs[:9], *nested)

    any_, vm, sm = pl.BlockSpec(memory_space=pl.ANY), pl.BlockSpec(memory_space=V), pl.BlockSpec(memory_space=pltpu.SMEM)
    encoded, attended = pl.pallas_call(
        body,
        out_shape=[jax.ShapeDtypeStruct((nresp, seq, 4 * HD), BF),
                   jax.ShapeDtypeStruct((npair, ntok, 4 * HD), BF)],
        in_specs=[any_, any_, any_, any_, sm, vm, vm],
        out_specs=[any_, any_],
        scratch_shapes=flat,
        compiler_params=pltpu.CompilerParams(
            collective_id=0, has_side_effects=True, vmem_limit_bytes=56 * 2 ** 20),
        name="judge",
    )(judge, hidden, w_query, w_keyval, lengths, pair_devices.T, pair_items.T)
    return copied(encoded, attended)


def solution(mesh):
    return jax.shard_map(
        on_device,
        mesh=mesh,
        in_specs=(
            P("dp", None, None),
            P("dp"),
            P("dp", None, "tensor"),
            P(None, "tensor"),
            P(None, "tensor"),
            P("dp", None),
            P("dp", None),
        ),
        out_specs=(P("dp", None, "tensor"), P("dp", None, "tensor")),
        check_vma=False,
    )
```

```python
import functools
import math
import jax
import jax.numpy as jnp
from jax import lax
from jax.experimental import pallas as pl
from jax.experimental.pallas import tpu as pltpu
from jax.sharding import PartitionSpec as P

HD = 128
C = 4
BF = jnp.bfloat16
F32 = jnp.float32
I32 = jnp.int32
MESH = pl.DeviceIdType.MESH
CAP_IN = HD ** -0.5 / 5.0
CAP_OUT = 5.0 * math.log2(math.e)

SCHED = (
    "KV0", "KV1", "KV2", "KV3", "XF0", "MY", "Q0", "MR", "Z0", "QP0",
    "XF1", "Y00", "Q1", "Z1", "QP1", "ML", "Y10", "XF2", "Q2", "MW",
    "Z2", "Y20", "XF3", "Q3", "Z3", "Y30", "QP2", "VP", "A00", "Y03",
    "Y02", "Y01", "A10", "A20", "Y13", "Y12", "Y11", "A03", "A30", "Y23",
    "Y22", "Y21", "A02", "A01", "Y33", "Y32", "Y31", "R00", "R10", "A13",
    "A12", "R20", "R30", "R03", "A11", "A23", "R02", "A22", "R01", "A21",
    "A33", "R13", "A32", "R12", "A31", "QP3", "R11", "R23", "R22", "R21",
    "SA0", "SA1", "R33", "R32", "R31", "SA2", "SA3", "H",
)


def weights_of(scores):
    return jnp.exp2(jnp.tanh(scores * CAP_IN) * CAP_OUT)


def kernel(judge, hidden, wq, wkv, lens, pdev, pitem, enc, pair, *scratch):
    (hid_v, wq_v, wkv_v, jin, jb, qself, kvx, vext, zs, ys, yq, rs, zr, mt, sm, smr, sm0, lt, ls,
     oenc, opair, lsem, ssem, rsem, qb, zq, yr, hret) = scratch
    npair, ntok, kslice = judge.shape
    tc = ntok // C
    rows = tc * 4
    per = rows // 16
    dp = lax.axis_index("dp")
    t = lax.axis_index("tensor")
    z, y = dp // 4, lax.rem(dp, 4)
    x, core = t // 2, lax.rem(t, 2)
    odd = lax.rem(z, 2)
    sg = 2 * odd - 1
    band = z // 2

    def mod(a, n):
        return lax.rem(a + 4 * n, n)

    zt = [z, mod(z + sg, 8), mod(z - 2 * sg, 8), mod(z + 3 * sg, 8)]
    zh = [z] + [mod(z + n * sg, 8) for n in (1, 2, 3)]

    def at(zz=None, yy=None, xx=None, cc=None):
        zz, yy = (z if zz is None else zz), (y if yy is None else yy)
        xx, cc = (x if xx is None else xx), (core if cc is None else cc)
        return (zz * 4 + yy, xx * 2 + cc)

    local_count = [0]
    recv_of, send_of, finals = {}, {}, []

    def remote(name, src, dst, dev, group, total):
        if group not in send_of:
            send_of[group] = len(send_of)
            finals.append((send_of[group], total))
        if name not in recv_of:
            recv_of[name] = len(recv_of)
        pltpu.make_async_remote_copy(
            src_ref=src, dst_ref=dst, send_sem=ssem.at[send_of[group]], recv_sem=rsem.at[recv_of[name]],
            device_id=dev, device_id_type=MESH).start()

    def arrived(name, dst):
        if name not in recv_of:
            recv_of[name] = len(recv_of)
        pltpu.make_async_remote_copy(
            src_ref=dst, dst_ref=dst, send_sem=ssem.at[0], recv_sem=rsem.at[recv_of[name]],
            device_id=(dp, t), device_id_type=MESH).wait_recv()

    def local(src, dst):
        copy = pltpu.make_async_copy(src, dst, lsem.at[local_count[0]])
        local_count[0] += 1
        copy.start()
        return copy

    l_j = local(judge, jin)
    l_kv = local(wkv, wkv_v)
    l_h = [local(hidden.at[r], hid_v.at[r]) for r in range(4)]
    l_q = local(wq, wq_v)

    barrier = pltpu.get_barrier_semaphore()
    peers = [at(xx=mod(x + d, 4)) for d in (1, 2, 3)] + [at(cc=1 - core)]
    peers += [at(yy=mod(y + d, 4)) for d in (1, 2, 3)]
    peers += [at(zz=mod(z + d, 8)) for d in (1, -1, 2, -2, 3, -3)]
    for dev in peers:
        pl.semaphore_signal(barrier, inc=1, device_id=dev, device_id_type=MESH)

    l_j.wait()
    def cut(c):
        part = jin[...].astype(F32)[:, c * tc:(c + 1) * tc, :]
        jb[c, t] = part.reshape(npair * tc, kslice).astype(BF)

    cut(0)
    pl.semaphore_wait(barrier, len(peers))

    xl, xr, x2 = mod(x - 1, 4), mod(x + 1, 4), mod(x + 2, 4)
    sl, sr, s2 = xl * 2 + core, xr * 2 + core, x2 * 2 + core
    sib = at(cc=1 - core)

    def xsend(name, c, slot, dev):
        remote(f"{name}{c}", jb.at[c, slot], jb.at[c, slot], dev, f"x{c}", jb.at[c, pl.ds(0, 7)])

    def X0(c):
        xsend("x2", c, t, at(xx=x2))
        xsend("xl", c, t, at(xx=xr))
        xsend("xr", c, t, at(xx=xl))
        xsend("sb", c, t, sib)

    def XF(c):
        for name, slot in (("xl", sl), ("xr", sr), ("x2", s2)):
            arrived(f"{name}{c}", jb.at[c, slot])
            xsend("sb", c, slot, sib)

    def piece(c, i):
        return jnp.dot(jb[c, i], wq_v[pl.ds(pl.multiple_of(i * kslice, kslice), kslice), :],
                       preferred_element_type=F32)

    def Q(c):
        q = piece(c, t) + piece(c, sl) + piece(c, sr) + piece(c, s2)
        arrived(f"sb{c}", jb.at[c, pl.ds(0, 4)])
        for slot in (t, sl, sr, s2):
            q = q + piece(c, slot + 1 - 2 * core)
        heads = [q[:, h * HD:(h + 1) * HD].reshape(npair, tc, HD) for h in range(4)]
        qb[c][...] = jnp.concatenate(heads, 1).astype(BF)

    def MZ():
        for n in (1, 2, 3):
            remote("mz", mt.at[y, 0], mt.at[y, n], at(zz=zt[n]), "mz", mt.at[y, pl.ds(0, 3)])
        remote("len", lt.at[odd], lt.at[odd], at(zz=z + 1 - 2 * odd), "len", lt.at[odd])

    late = []

    def MY():
        arrived("mz", mt.at[y, pl.ds(1, 3)])
        for d in (1, 2, 3):
            remote("my", mt.at[y], mt.at[y], at(yy=mod(y + d, 4)), "my", mt.at[pl.ds(0, 3)])
        late.append(local(mt.at[y], smr))

    def ML():
        arrived("my", mt.at[pl.ds(0, 3)])
        arrived("len", lt.at[1 - odd])
        late.append(local(mt, sm))
        late.append(local(lt, ls))

    def MR():
        late[0].wait()

    def MW():
        late[1].wait()
        late[2].wait()

    def masked(v, length):
        keys = lax.broadcasted_iota(I32, (v.shape[0], 2 * HD), 0)
        both = jnp.concatenate([v.astype(F32), jnp.ones(v.shape, F32)], 1)
        return jnp.where(keys < length, both, 0.0).astype(BF)

    def KV(r):
        if r == 0:
            l_kv.wait()
        l_h[r].wait()
        kv = jnp.dot(hid_v[r], wkv_v[...], preferred_element_type=F32).astype(BF)
        kvx[odd, r, 0] = kv[:, :HD]
        kvx[odd, r, 1] = kv[:, HD:]
        vext[odd, r] = masked(kv[:, HD:], lens[r])
        remote("kv", kvx.at[odd, r], kvx.at[odd, r], at(zz=z + 1 - 2 * odd),
               "kv", kvx.at[odd])

    def VP():
        other = 1 - odd
        arrived("kv", kvx.at[other])

        def one(r, carry):
            vext[other, r] = masked(kvx[other, r, 1], ls[other, 0, r])
            return carry

        lax.fori_loop(0, 4, one, 0)

    def QP(r):
        q = jnp.dot(hid_v[r], wq_v[...], preferred_element_type=F32).astype(BF)
        for h in range(4):
            qself[r, h] = q[:, h * HD:(h + 1) * HD]

    enc_out = []

    def SA(r):
        k_r = kvx[odd, r, 0]
        v_r = vext[odd, r]
        for h in range(4):
            for b in range(2):
                n = (b + 1) * 128
                s = lax.dot_general(qself[r, h, b * 128:(b + 1) * 128, :], k_r[:n],
                                    (((1,), (1,)), ((), ())), preferred_element_type=F32)
                qi = lax.broadcasted_iota(I32, (128, n), 0) + b * 128
                ti = lax.broadcasted_iota(I32, (128, n), 1)
                w = jnp.where(ti <= qi, weights_of(s), 0.0).astype(BF)
                ne = jnp.dot(w, v_r[:n], preferred_element_type=F32)
                oenc[r, b * 128:(b + 1) * 128, h * HD:(h + 1) * HD] = (
                    ne[:, :HD] / ne[:, HD:]).astype(BF)
        enc_out.append(local(oenc.at[r], enc.at[r]))

    def Z(c):
        for n in (3, 2, 1, 0):
            for k in range(8):
                block = qb[c][jnp.bitwise_and(sm0[4, n * 8 + k], npair - 1)]
                if n:
                    zs[c, n - 1, k] = block
                else:
                    zq[c][0][k] = block
            if n:
                remote(f"z{c}{n}", zs.at[c, n - 1], zq[c][n], at(zz=zt[n]), f"z{c}", zs.at[c])

    def Y(c, n):
        if n:
            arrived(f"z{c}{n}", zq[c][n])
        tile = smr.at[n] if n else sm0
        for d in (2, 1, 3, 0):
            yy = mod(y + d, 4)
            for s in range(4):
                which = jnp.bitwise_and(tile[s % 2, (2 * band + s // 2) * 4 + yy], 7)
                block = zq[c][n][which]
                if d:
                    ys[c, n, d - 1, s] = block
                else:
                    yq[c, n, y, s] = block
            if d:
                remote(f"y{c}{n}", ys.at[c, n, d - 1], yq.at[c, n, y], at(yy=yy), f"y{c}", ys.at[c])

    diag = lax.broadcasted_iota(I32, (rows, 128), 0) == lax.broadcasted_iota(I32, (rows, 128), 1)
    sub16 = lax.broadcasted_iota(I32, (16, 128), 0)

    def A(c, n):
        arrived(f"y{c}{n}", yq.at[c, n, pl.ds(0, 3)])

        def one(src, carry):
            dens = []
            for s in range(4):
                zz, j = s // 2, s % 2
                it = jnp.bitwise_and(sm[src, n, 2 + j, (2 * band + zz) * 4 + y], 3)
                sc = lax.dot_general(yq[c, n, src, s], kvx[zz, it, 0],
                                     (((1,), (1,)), ((), ())), preferred_element_type=F32)
                ne = jnp.dot(weights_of(sc).astype(BF), vext[zz, it], preferred_element_type=F32)
                rs[c, n, src, s * per:(s + 1) * per] = ne[:, :HD].astype(BF).reshape(per, 16, HD)
                dens.append(jnp.sum(jnp.where(diag, ne[:, HD:], 0.0), 0, keepdims=True))
            den = jnp.concatenate(dens, 0)
            high = den.astype(BF).astype(F32)
            rs[c, n, src, 4 * per] = jnp.concatenate(
                [high, den - high, jnp.zeros((8, 128), F32)], 0).astype(BF)
            return carry

        lax.fori_loop(0, 4, one, 0, unroll=4)
        for d in (2, 1, 3):
            yy = mod(y + d, 4)
            remote(f"r{c}{n}", rs.at[c, n, yy], yr[c][n].at[y], at(yy=yy), f"r{c}", rs.at[c, pl.ds(0, 3)])
        yr[c][n][y] = rs[c, n, y]

    def R(c, n):
        arrived(f"r{c}{n}", yr[c][n].at[pl.ds(0, 3)])
        tile = smr.at[n] if n else sm0
        for k in range(8):
            num, den = [], []
            for side in (0, 1):
                p = jnp.bitwise_and(tile[5 + side, n * 8 + k], 15)
                src, s = p // 4, lax.rem(p, 4)
                num.append(yr[c][n][src, pl.ds(s * per, per)].reshape(rows, HD).astype(F32))
                dens = yr[c][n][src, 4 * per].astype(F32)
                den.append(jnp.where((sub16 == s) | (sub16 == s + 4), dens, 0.0))
            total = jnp.sum(den[0] + den[1], 0, keepdims=True)
            total = jnp.sum(jnp.where(diag, total, 0.0), 1, keepdims=True)
            block = ((num[0] + num[1]) / total).astype(BF)
            if n:
                zr[c, n - 1, k] = block
            else:
                hret[c][k] = block
        if n:
            remote(f"h{c}", zr.at[c, n - 1], hret[c].at[pl.ds(n * 8, 8)], at(zz=zh[n]), f"h{c}", zr.at[c])

    def H():
        for c in range(C):
            arrived(f"h{c}", hret[c].at[pl.ds(8, 24)])
        for p in range(npair):
            spot_p = jnp.bitwise_and(sm0[7, p], 31)
            got = [hret[c][spot_p].astype(F32) for c in range(C)]
            for h in range(4):
                opair[p, :, h * HD:(h + 1) * HD] = jnp.concatenate(
                    [g[h * tc:(h + 1) * tc] for g in got], 0).astype(BF)
        enc_out.append(local(opair, pair))

    for c in range(C):
        if c:
            cut(c)
        X0(c)

    lane = lax.broadcasted_iota(I32, (npair, 128), 1)
    sub = lax.broadcasted_iota(I32, (npair, 128), 0)
    eye = lax.broadcasted_iota(I32, (npair, npair), 0) == lax.broadcasted_iota(I32, (npair, npair), 1)

    def column(row):
        return jnp.sum(jnp.where(eye, row, 0), 1, keepdims=True)

    dev0, dev1, item = column(pdev[0:1, :]), column(pdev[1:2, :]), column(pitem[0:1, :])
    strict = jnp.where(
        lax.broadcasted_iota(I32, (npair, npair), 1) < lax.broadcasted_iota(I32, (npair, npair), 0),
        1.0, 0.0).astype(F32)
    m0 = jnp.where(dev0 == lane, 1.0, 0.0)
    m1 = jnp.where(dev1 == lane, 1.0, 0.0)
    m = m0 + m1
    rank = jnp.dot(strict, m, preferred_element_type=F32)
    rel = jnp.bitwise_and(lax.shift_right_logical(dev0, 3) - band + 4, 3)
    near = jnp.where(rel == 0, 0, jnp.where(rel == 2, 3, jnp.where((rel == 1) == (odd == 1), 1, 2)))
    mb = jnp.where(near == lane, 1.0, 0.0)
    place = jnp.sum(mb * jnp.dot(strict, mb, preferred_element_type=F32), 1, keepdims=True)
    home = near.astype(F32) * 8.0 + place
    at_home = jnp.where(home == lane.astype(F32), 1.0, 0.0)

    def down(v):
        return jnp.sum(v, 0, keepdims=True)

    first = jnp.where(rank == 0.0, m, 0.0)
    second = jnp.where(rank == 1.0, m, 0.0)
    spot = (jnp.bitwise_and(lane, 3) * 4
            + jnp.bitwise_and(lax.shift_right_logical(lane, 2), 1) * 2).astype(F32) + rank
    pos0 = jnp.sum(m0 * spot, 1, keepdims=True)
    pos1 = jnp.sum(m1 * spot, 1, keepdims=True)
    itemf = item.astype(F32)
    subf = sub.astype(F32)
    table = jnp.concatenate([
        down(first * place), down(second * place), down(first * itemf), down(second * itemf),
        down(at_home * subf), down(at_home * pos0), down(at_home * pos1),
        down(jnp.where(sub == lane, home, 0.0))], 0)
    mt[y, 0] = table.astype(I32)
    l_0 = local(mt.at[y, 0], sm0)
    lane8 = lax.broadcasted_iota(I32, (8, 128), 1)
    lt[odd] = jnp.where(lane8 == 0, lens[0], jnp.where(lane8 == 1, lens[1],
                        jnp.where(lane8 == 2, lens[2], lens[3])))

    MZ()
    stages = {"XF": XF, "MR": MR, "MW": MW, "Q": Q, "KV": KV, "QP": QP, "SA": SA, "Z": Z, "Y": Y, "A": A,
              "R": R, "MY": MY, "ML": ML, "VP": VP, "H": H}
    waited = []
    for word in SCHED:
        name = word.rstrip("0123456789")
        if name in ("Q", "QP") and not waited:
            l_q.wait()
            l_0.wait()
            waited.append(word)
        stages[name](*[int(d) for d in word[len(name):]])
    for copy in enc_out:
        copy.wait()
    for slot, total in finals:
        pltpu.make_async_remote_copy(
            src_ref=total, dst_ref=total, send_sem=ssem.at[slot], recv_sem=rsem.at[0],
            device_id=(dp, t), device_id_type=MESH).wait_send()


def copy_kernel(enc, pair, enc_out, pair_out, enc_v, pair_v, sem):
    steps = [(enc.at[r], enc_v.at[r], enc_out.at[r]) for r in range(4)] + [(pair, pair_v, pair_out)]
    inward = [pltpu.make_async_copy(src, mid, sem.at[k]) for k, (src, mid, _) in enumerate(steps)]
    outward = [pltpu.make_async_copy(mid, dst, sem.at[5 + k]) for k, (_, mid, dst) in enumerate(steps)]
    for copy in inward:
        copy.start()
    for first, second in zip(inward, outward):
        first.wait()
        second.start()
    for copy in outward:
        copy.wait()


def copied(encoded, attended):
    spec = pl.BlockSpec(memory_space=pl.ANY)
    return pl.pallas_call(
        copy_kernel,
        out_shape=[jax.ShapeDtypeStruct(a.shape, a.dtype) for a in (encoded, attended)],
        in_specs=[spec, spec], out_specs=[spec, spec],
        scratch_shapes=[pltpu.VMEM(encoded.shape, BF), pltpu.VMEM(attended.shape, BF),
                        pltpu.SemaphoreType.DMA((10,))],
        name="results",
    )(encoded, attended)


def on_device(hidden, lengths, judge, w_query, w_keyval, pair_devices, pair_items):
    npair, ntok, kslice = judge.shape
    nresp, seq, width = hidden.shape
    rows = ntok // C * 4
    V = pltpu.VMEM
    scratch = [
        V((nresp, seq, width), BF), V(w_query.shape, BF), V(w_keyval.shape, BF), V(judge.shape, BF),
        V((C, 8, npair * ntok // C, kslice), BF), V((nresp, 4, seq, HD), BF),
        V((2, 4, 2, seq, HD), BF), V((2, 4, seq, 2 * HD), BF),
        V((C, 3, 8, rows, HD), BF), V((C, 4, 3, 4, rows, HD), BF), V((C, 4, 4, 4, rows, HD), BF),
        V((C, 4, 4, rows // 4 + 1, 16, HD), BF), V((C, 3, 8, rows, HD), BF),
        V((4, 4, 8, 128), I32), pltpu.SMEM((4, 4, 8, 128), I32), pltpu.SMEM((4, 8, 128), I32), pltpu.SMEM((8, 128), I32),
        V((2, 8, 128), I32), pltpu.SMEM((2, 8, 128), I32),
        V((nresp, seq, 4 * HD), BF), V((npair, ntok, 4 * HD), BF),
        pltpu.SemaphoreType.DMA((16,)), pltpu.SemaphoreType.DMA((5 * C + 4,)), pltpu.SemaphoreType.DMA((16 * C + 4,)),
        [V((npair, rows, HD), BF) for _ in range(C)],
        [[V((8, rows, HD), BF) for _ in range(4)] for _ in range(C)],
        [[V((4, rows // 4 + 1, 16, HD), BF) for _ in range(4)] for _ in range(C)],
        [V((32, rows, HD), BF) for _ in range(C)],
    ]
    flat, tree = jax.tree.flatten(scratch, is_leaf=lambda s: not isinstance(s, list))

    def body(*refs):
        nested = jax.tree.unflatten(tree, refs[9:])
        kernel(*refs[:9], *nested)

    any_, vm, sm = pl.BlockSpec(memory_space=pl.ANY), pl.BlockSpec(memory_space=V), pl.BlockSpec(memory_space=pltpu.SMEM)
    encoded, attended = pl.pallas_call(
        body,
        out_shape=[jax.ShapeDtypeStruct((nresp, seq, 4 * HD), BF),
                   jax.ShapeDtypeStruct((npair, ntok, 4 * HD), BF)],
        in_specs=[any_, any_, any_, any_, sm, vm, vm],
        out_specs=[any_, any_],
        scratch_shapes=flat,
        compiler_params=pltpu.CompilerParams(
            collective_id=0, has_side_effects=True, vmem_limit_bytes=56 * 2 ** 20),
        name="judge",
    )(judge, hidden, w_query, w_keyval, lengths, pair_devices.T, pair_items.T)
    return copied(encoded, attended)


def solution(mesh):
    return jax.shard_map(
        on_device,
        mesh=mesh,
        in_specs=(
            P("dp", None, None),
            P("dp"),
            P("dp", None, "tensor"),
            P(None, "tensor"),
            P(None, "tensor"),
            P("dp", None),
            P("dp", None),
        ),
        out_specs=(P("dp", None, "tensor"), P("dp", None, "tensor")),
        check_vma=False,
    )
```

```python
import functools
import math
import jax
import jax.numpy as jnp
from jax import lax
from jax.experimental import pallas as pl
from jax.experimental.pallas import tpu as pltpu
from jax.sharding import PartitionSpec as P

HD = 128
C = 4
BF = jnp.bfloat16
F32 = jnp.float32
I32 = jnp.int32
MESH = pl.DeviceIdType.MESH
CAP_IN = HD ** -0.5 / 5.0
CAP_OUT = 5.0 * math.log2(math.e)

SCHED = (
    "KV0", "KV1", "KV2", "KV3", "XF0", "MY", "Q0", "MR", "Z0", "QP0",
    "XF1", "Y00", "Q1", "Z1", "QP1", "ML", "Y10", "XF2", "Q2", "MW",
    "Z2", "Y20", "XF3", "Q3", "Z3", "Y30", "QP2", "VP", "A00", "Y03",
    "Y02", "Y01", "A10", "A20", "Y13", "Y12", "Y11", "A03", "A30", "Y23",
    "Y22", "Y21", "A02", "A01", "Y33", "Y32", "Y31", "R00", "R10", "A13",
    "A12", "R20", "R30", "R03", "A11", "A23", "R02", "A22", "R01", "A21",
    "A33", "R13", "A32", "R12", "A31", "R11", "R23", "R22", "R21", "SA0",
    "SA1", "R33", "R32", "R31", "QP3", "SA2", "SA3", "H",
)


def weights_of(scores):
    return jnp.exp2(jnp.tanh(scores * CAP_IN) * CAP_OUT)


def kernel(judge, hidden, wq, wkv, lens, pdev, pitem, enc, pair, *scratch):
    (hid_v, wq_v, wkv_v, jin, jb, qself, kvx, vext, zs, ys, yq, rs, zr, mt, sm, smr, sm0, lt, ls,
     oenc, opair, lsem, ssem, rsem, qb, zq, yr, hret) = scratch
    npair, ntok, kslice = judge.shape
    tc = ntok // C
    rows = tc * 4
    per = rows // 16
    dp = lax.axis_index("dp")
    t = lax.axis_index("tensor")
    z, y = dp // 4, lax.rem(dp, 4)
    x, core = t // 2, lax.rem(t, 2)
    odd = lax.rem(z, 2)
    sg = 2 * odd - 1
    band = z // 2

    def mod(a, n):
        return lax.rem(a + 4 * n, n)

    zt = [z, mod(z + sg, 8), mod(z - 2 * sg, 8), mod(z + 3 * sg, 8)]
    zh = [z] + [mod(z + n * sg, 8) for n in (1, 2, 3)]

    def at(zz=None, yy=None, xx=None, cc=None):
        zz, yy = (z if zz is None else zz), (y if yy is None else yy)
        xx, cc = (x if xx is None else xx), (core if cc is None else cc)
        return (zz * 4 + yy, xx * 2 + cc)

    local_count = [0]
    recv_of, send_of, finals = {}, {}, []

    def remote(name, src, dst, dev, group, total):
        if group not in send_of:
            send_of[group] = len(send_of)
            finals.append((send_of[group], total))
        if name not in recv_of:
            recv_of[name] = len(recv_of)
        pltpu.make_async_remote_copy(
            src_ref=src, dst_ref=dst, send_sem=ssem.at[send_of[group]], recv_sem=rsem.at[recv_of[name]],
            device_id=dev, device_id_type=MESH).start()

    def arrived(name, dst):
        if name not in recv_of:
            recv_of[name] = len(recv_of)
        pltpu.make_async_remote_copy(
            src_ref=dst, dst_ref=dst, send_sem=ssem.at[0], recv_sem=rsem.at[recv_of[name]],
            device_id=(dp, t), device_id_type=MESH).wait_recv()

    def local(src, dst):
        copy = pltpu.make_async_copy(src, dst, lsem.at[local_count[0]])
        local_count[0] += 1
        copy.start()
        return copy

    l_j = local(judge, jin)
    l_kv = local(wkv, wkv_v)
    l_h = [local(hidden.at[r], hid_v.at[r]) for r in range(4)]
    l_q = local(wq, wq_v)

    barrier = pltpu.get_barrier_semaphore()
    peers = [at(xx=mod(x + d, 4)) for d in (1, 2, 3)] + [at(cc=1 - core)]
    peers += [at(yy=mod(y + d, 4)) for d in (1, 2, 3)]
    peers += [at(zz=mod(z + d, 8)) for d in (1, -1, 2, -2, 3, -3)]
    for dev in peers:
        pl.semaphore_signal(barrier, inc=1, device_id=dev, device_id_type=MESH)

    l_j.wait()
    def cut(c):
        part = jin[...].astype(F32)[:, c * tc:(c + 1) * tc, :]
        jb[c, t] = part.reshape(npair * tc, kslice).astype(BF)

    cut(0)
    pl.semaphore_wait(barrier, len(peers))

    xl, xr, x2 = mod(x - 1, 4), mod(x + 1, 4), mod(x + 2, 4)
    sl, sr, s2 = xl * 2 + core, xr * 2 + core, x2 * 2 + core
    sib = at(cc=1 - core)

    def xsend(name, c, slot, dev):
        remote(f"{name}{c}", jb.at[c, slot], jb.at[c, slot], dev, f"x{c}", jb.at[c, pl.ds(0, 7)])

    def X0(c):
        xsend("x2", c, t, at(xx=x2))
        xsend("xl", c, t, at(xx=xr))
        xsend("xr", c, t, at(xx=xl))
        xsend("sb", c, t, sib)

    def XF(c):
        for name, slot in (("xl", sl), ("xr", sr), ("x2", s2)):
            arrived(f"{name}{c}", jb.at[c, slot])
            xsend("sb", c, slot, sib)

    def piece(c, i):
        return jnp.dot(jb[c, i], wq_v[pl.ds(pl.multiple_of(i * kslice, kslice), kslice), :],
                       preferred_element_type=F32)

    def Q(c):
        q = piece(c, t) + piece(c, sl) + piece(c, sr) + piece(c, s2)
        arrived(f"sb{c}", jb.at[c, pl.ds(0, 4)])
        for slot in (t, sl, sr, s2):
            q = q + piece(c, slot + 1 - 2 * core)
        heads = [q[:, h * HD:(h + 1) * HD].reshape(npair, tc, HD) for h in range(4)]
        qb[c][...] = jnp.concatenate(heads, 1).astype(BF)

    def MZ():
        for n in (1, 2, 3):
            remote("mz", mt.at[y, 0], mt.at[y, n], at(zz=zt[n]), "mz", mt.at[y, pl.ds(0, 3)])
        remote("len", lt.at[odd], lt.at[odd], at(zz=z + 1 - 2 * odd), "len", lt.at[odd])

    late = []

    def MY():
        arrived("mz", mt.at[y, pl.ds(1, 3)])
        for d in (1, 2, 3):
            remote("my", mt.at[y], mt.at[y], at(yy=mod(y + d, 4)), "my", mt.at[pl.ds(0, 3)])
        late.append(local(mt.at[y], smr))

    def ML():
        arrived("my", mt.at[pl.ds(0, 3)])
        arrived("len", lt.at[1 - odd])
        late.append(local(mt, sm))
        late.append(local(lt, ls))

    def MR():
        late[0].wait()

    def MW():
        late[1].wait()
        late[2].wait()

    def masked(v, length):
        keys = lax.broadcasted_iota(I32, (v.shape[0], 2 * HD), 0)
        both = jnp.concatenate([v.astype(F32), jnp.ones(v.shape, F32)], 1)
        return jnp.where(keys < length, both, 0.0).astype(BF)

    def KV(r):
        if r == 0:
            l_kv.wait()
        l_h[r].wait()
        kv = jnp.dot(hid_v[r], wkv_v[...], preferred_element_type=F32).astype(BF)
        kvx[odd, r, 0] = kv[:, :HD]
        kvx[odd, r, 1] = kv[:, HD:]
        vext[odd, r] = masked(kv[:, HD:], lens[r])
        remote("kv", kvx.at[odd, r], kvx.at[odd, r], at(zz=z + 1 - 2 * odd),
               "kv", kvx.at[odd])

    def VP():
        other = 1 - odd
        arrived("kv", kvx.at[other])

        def one(r, carry):
            vext[other, r] = masked(kvx[other, r, 1], ls[other, 0, r])
            return carry

        lax.fori_loop(0, 4, one, 0)

    def QP(r):
        q = jnp.dot(hid_v[r], wq_v[...], preferred_element_type=F32).astype(BF)
        for h in range(4):
            qself[r, h] = q[:, h * HD:(h + 1) * HD]

    enc_out = []

    def SA(r):
        k_r = kvx[odd, r, 0]
        v_r = vext[odd, r]
        for h in range(4):
            for b in range(2):
                n = (b + 1) * 128
                s = lax.dot_general(qself[r, h, b * 128:(b + 1) * 128, :], k_r[:n],
                                    (((1,), (1,)), ((), ())), preferred_element_type=F32)
                qi = lax.broadcasted_iota(I32, (128, n), 0) + b * 128
                ti = lax.broadcasted_iota(I32, (128, n), 1)
                w = jnp.where(ti <= qi, weights_of(s), 0.0).astype(BF)
                ne = jnp.dot(w, v_r[:n], preferred_element_type=F32)
                oenc[r, b * 128:(b + 1) * 128, h * HD:(h + 1) * HD] = (
                    ne[:, :HD] / ne[:, HD:]).astype(BF)
        enc_out.append(local(oenc.at[r], enc.at[r]))

    def Z(c):
        for n in (3, 2, 1, 0):
            for k in range(8):
                block = qb[c][jnp.bitwise_and(sm0[4, n * 8 + k], npair - 1)]
                if n:
                    zs[c, n - 1, k] = block
                else:
                    zq[c][0][k] = block
            if n:
                remote(f"z{c}{n}", zs.at[c, n - 1], zq[c][n], at(zz=zt[n]), f"z{c}", zs.at[c])

    def Y(c, n):
        if n:
            arrived(f"z{c}{n}", zq[c][n])
        tile = smr.at[n] if n else sm0
        for d in (2, 1, 3, 0):
            yy = mod(y + d, 4)
            for s in range(4):
                which = jnp.bitwise_and(tile[s % 2, (2 * band + s // 2) * 4 + yy], 7)
                block = zq[c][n][which]
                if d:
                    ys[c, n, d - 1, s] = block
                else:
                    yq[c, n, y, s] = block
            if d:
                remote(f"y{c}{n}", ys.at[c, n, d - 1], yq.at[c, n, y], at(yy=yy), f"y{c}", ys.at[c])

    diag = lax.broadcasted_iota(I32, (rows, 128), 0) == lax.broadcasted_iota(I32, (rows, 128), 1)
    sub16 = lax.broadcasted_iota(I32, (16, 128), 0)

    def A(c, n):
        arrived(f"y{c}{n}", yq.at[c, n, pl.ds(0, 3)])

        def one(src, carry):
            dens = []
            for s in range(4):
                zz, j = s // 2, s % 2
                it = jnp.bitwise_and(sm[src, n, 2 + j, (2 * band + zz) * 4 + y], 3)
                sc = lax.dot_general(yq[c, n, src, s], kvx[zz, it, 0],
                                     (((1,), (1,)), ((), ())), preferred_element_type=F32)
                ne = jnp.dot(weights_of(sc).astype(BF), vext[zz, it], preferred_element_type=F32)
                rs[c, n, src, s * per:(s + 1) * per] = ne[:, :HD].astype(BF).reshape(per, 16, HD)
                dens.append(jnp.sum(jnp.where(diag, ne[:, HD:], 0.0), 0, keepdims=True))
            den = jnp.concatenate(dens, 0)
            high = den.astype(BF).astype(F32)
            rs[c, n, src, 4 * per] = jnp.concatenate(
                [high, den - high, jnp.zeros((8, 128), F32)], 0).astype(BF)
            return carry

        lax.fori_loop(0, 4, one, 0, unroll=4)
        for d in (2, 1, 3):
            yy = mod(y + d, 4)
            remote(f"r{c}{n}", rs.at[c, n, yy], yr[c][n].at[y], at(yy=yy), f"r{c}", rs.at[c, pl.ds(0, 3)])
        yr[c][n][y] = rs[c, n, y]

    def R(c, n):
        arrived(f"r{c}{n}", yr[c][n].at[pl.ds(0, 3)])
        tile = smr.at[n] if n else sm0
        for k in range(8):
            num, den = [], []
            for side in (0, 1):
                p = jnp.bitwise_and(tile[5 + side, n * 8 + k], 15)
                src, s = p // 4, lax.rem(p, 4)
                num.append(yr[c][n][src, pl.ds(s * per, per)].reshape(rows, HD).astype(F32))
                dens = yr[c][n][src, 4 * per].astype(F32)
                den.append(jnp.where((sub16 == s) | (sub16 == s + 4), dens, 0.0))
            total = jnp.sum(den[0] + den[1], 0, keepdims=True)
            total = jnp.sum(jnp.where(diag, total, 0.0), 1, keepdims=True)
            block = ((num[0] + num[1]) / total).astype(BF)
            if n:
                zr[c, n - 1, k] = block
            else:
                hret[c][k] = block
        if n:
            remote(f"h{c}", zr.at[c, n - 1], hret[c].at[pl.ds(n * 8, 8)], at(zz=zh[n]), f"h{c}", zr.at[c])

    def H():
        for c in range(C):
            arrived(f"h{c}", hret[c].at[pl.ds(8, 24)])
        for p in range(npair):
            spot_p = jnp.bitwise_and(sm0[7, p], 31)
            got = [hret[c][spot_p].astype(F32) for c in range(C)]
            for h in range(4):
                opair[p, :, h * HD:(h + 1) * HD] = jnp.concatenate(
                    [g[h * tc:(h + 1) * tc] for g in got], 0).astype(BF)
        enc_out.append(local(opair, pair))

    for c in range(C):
        if c:
            cut(c)
        X0(c)

    lane = lax.broadcasted_iota(I32, (npair, 128), 1)
    sub = lax.broadcasted_iota(I32, (npair, 128), 0)
    eye = lax.broadcasted_iota(I32, (npair, npair), 0) == lax.broadcasted_iota(I32, (npair, npair), 1)

    def column(row):
        return jnp.sum(jnp.where(eye, row, 0), 1, keepdims=True)

    dev0, dev1, item = column(pdev[0:1, :]), column(pdev[1:2, :]), column(pitem[0:1, :])
    strict = jnp.where(
        lax.broadcasted_iota(I32, (npair, npair), 1) < lax.broadcasted_iota(I32, (npair, npair), 0),
        1.0, 0.0).astype(F32)
    m0 = jnp.where(dev0 == lane, 1.0, 0.0)
    m1 = jnp.where(dev1 == lane, 1.0, 0.0)
    m = m0 + m1
    rank = jnp.dot(strict, m, preferred_element_type=F32)
    rel = jnp.bitwise_and(lax.shift_right_logical(dev0, 3) - band + 4, 3)
    near = jnp.where(rel == 0, 0, jnp.where(rel == 2, 3, jnp.where((rel == 1) == (odd == 1), 1, 2)))
    mb = jnp.where(near == lane, 1.0, 0.0)
    place = jnp.sum(mb * jnp.dot(strict, mb, preferred_element_type=F32), 1, keepdims=True)
    home = near.astype(F32) * 8.0 + place
    at_home = jnp.where(home == lane.astype(F32), 1.0, 0.0)

    def down(v):
        return jnp.sum(v, 0, keepdims=True)

    first = jnp.where(rank == 0.0, m, 0.0)
    second = jnp.where(rank == 1.0, m, 0.0)
    spot = (jnp.bitwise_and(lane, 3) * 4
            + jnp.bitwise_and(lax.shift_right_logical(lane, 2), 1) * 2).astype(F32) + rank
    pos0 = jnp.sum(m0 * spot, 1, keepdims=True)
    pos1 = jnp.sum(m1 * spot, 1, keepdims=True)
    itemf = item.astype(F32)
    subf = sub.astype(F32)
    table = jnp.concatenate([
        down(first * place), down(second * place), down(first * itemf), down(second * itemf),
        down(at_home * subf), down(at_home * pos0), down(at_home * pos1),
        down(jnp.where(sub == lane, home, 0.0))], 0)
    mt[y, 0] = table.astype(I32)
    l_0 = local(mt.at[y, 0], sm0)
    lane8 = lax.broadcasted_iota(I32, (8, 128), 1)
    lt[odd] = jnp.where(lane8 == 0, lens[0], jnp.where(lane8 == 1, lens[1],
                        jnp.where(lane8 == 2, lens[2], lens[3])))

    MZ()
    stages = {"XF": XF, "MR": MR, "MW": MW, "Q": Q, "KV": KV, "QP": QP, "SA": SA, "Z": Z, "Y": Y, "A": A,
              "R": R, "MY": MY, "ML": ML, "VP": VP, "H": H}
    waited = []
    for word in SCHED:
        name = word.rstrip("0123456789")
        if name in ("Q", "QP") and not waited:
            l_q.wait()
            l_0.wait()
            waited.append(word)
        stages[name](*[int(d) for d in word[len(name):]])
    for copy in enc_out:
        copy.wait()
    for slot, total in finals:
        pltpu.make_async_remote_copy(
            src_ref=total, dst_ref=total, send_sem=ssem.at[slot], recv_sem=rsem.at[0],
            device_id=(dp, t), device_id_type=MESH).wait_send()


def copy_kernel(enc, pair, enc_out, pair_out, enc_v, pair_v, sem):
    steps = [(enc.at[r], enc_v.at[r], enc_out.at[r]) for r in range(4)] + [(pair, pair_v, pair_out)]
    inward = [pltpu.make_async_copy(src, mid, sem.at[k]) for k, (src, mid, _) in enumerate(steps)]
    outward = [pltpu.make_async_copy(mid, dst, sem.at[5 + k]) for k, (_, mid, dst) in enumerate(steps)]
    for copy in inward:
        copy.start()
    for first, second in zip(inward, outward):
        first.wait()
        second.start()
    for copy in outward:
        copy.wait()


def copied(encoded, attended):
    spec = pl.BlockSpec(memory_space=pl.ANY)
    return pl.pallas_call(
        copy_kernel,
        out_shape=[jax.ShapeDtypeStruct(a.shape, a.dtype) for a in (encoded, attended)],
        in_specs=[spec, spec], out_specs=[spec, spec],
        scratch_shapes=[pltpu.VMEM(encoded.shape, BF), pltpu.VMEM(attended.shape, BF),
                        pltpu.SemaphoreType.DMA((10,))],
        name="results",
    )(encoded, attended)


def on_device(hidden, lengths, judge, w_query, w_keyval, pair_devices, pair_items):
    npair, ntok, kslice = judge.shape
    nresp, seq, width = hidden.shape
    rows = ntok // C * 4
    V = pltpu.VMEM
    scratch = [
        V((nresp, seq, width), BF), V(w_query.shape, BF), V(w_keyval.shape, BF), V(judge.shape, BF),
        V((C, 8, npair * ntok // C, kslice), BF), V((nresp, 4, seq, HD), BF),
        V((2, 4, 2, seq, HD), BF), V((2, 4, seq, 2 * HD), BF),
        V((C, 3, 8, rows, HD), BF), V((C, 4, 3, 4, rows, HD), BF), V((C, 4, 4, 4, rows, HD), BF),
        V((C, 4, 4, rows // 4 + 1, 16, HD), BF), V((C, 3, 8, rows, HD), BF),
        V((4, 4, 8, 128), I32), pltpu.SMEM((4, 4, 8, 128), I32), pltpu.SMEM((4, 8, 128), I32), pltpu.SMEM((8, 128), I32),
        V((2, 8, 128), I32), pltpu.SMEM((2, 8, 128), I32),
        V((nresp, seq, 4 * HD), BF), V((npair, ntok, 4 * HD), BF),
        pltpu.SemaphoreType.DMA((16,)), pltpu.SemaphoreType.DMA((5 * C + 4,)), pltpu.SemaphoreType.DMA((16 * C + 4,)),
        [V((npair, rows, HD), BF) for _ in range(C)],
        [[V((8, rows, HD), BF) for _ in range(4)] for _ in range(C)],
        [[V((4, rows // 4 + 1, 16, HD), BF) for _ in range(4)] for _ in range(C)],
        [V((32, rows, HD), BF) for _ in range(C)],
    ]
    flat, tree = jax.tree.flatten(scratch, is_leaf=lambda s: not isinstance(s, list))

    def body(*refs):
        nested = jax.tree.unflatten(tree, refs[9:])
        kernel(*refs[:9], *nested)

    any_, vm, sm = pl.BlockSpec(memory_space=pl.ANY), pl.BlockSpec(memory_space=V), pl.BlockSpec(memory_space=pltpu.SMEM)
    encoded, attended = pl.pallas_call(
        body,
        out_shape=[jax.ShapeDtypeStruct((nresp, seq, 4 * HD), BF),
                   jax.ShapeDtypeStruct((npair, ntok, 4 * HD), BF)],
        in_specs=[any_, any_, any_, any_, sm, vm, vm],
        out_specs=[any_, any_],
        scratch_shapes=flat,
        compiler_params=pltpu.CompilerParams(
            collective_id=0, has_side_effects=True, vmem_limit_bytes=56 * 2 ** 20),
        name="judge",
    )(judge, hidden, w_query, w_keyval, lengths, pair_devices.T, pair_items.T)
    return copied(encoded, attended)


def solution(mesh):
    return jax.shard_map(
        on_device,
        mesh=mesh,
        in_specs=(
            P("dp", None, None),
            P("dp"),
            P("dp", None, "tensor"),
            P(None, "tensor"),
            P(None, "tensor"),
            P("dp", None),
            P("dp", None),
        ),
        out_specs=(P("dp", None, "tensor"), P("dp", None, "tensor")),
        check_vma=False,
    )
```
